256 devices in a mesh: pipe: 2 (over core), dp: 128 (over z, y, x).
Axes of the slice: x: 4, y: 4, z: 8, core: 2. Of those that a mesh axis runs over, the one named last changes fastest.
Arguments:
- tiles: bfloat16 [2, 128, 16, 8, 2048], P(None, 'dp'), may hold values from -6 to 6
- counts: int32 [2, 128], P(None, 'dp'), may hold values from 1 to 16, 512 in all within a row
- cells: int32 [2, 128, 16], P(None, 'dp'), may hold values from 0 to 255, as said below
- block_in: bfloat16 [2, 2048, 512], P('pipe'), may hold values from -0.125 to 0.125
- block_out: bfloat16 [2, 512, 2048], P('pipe'), may hold values from -0.25 to 0.25
- proj: bfloat16 [2048, 1536], P(None, 'pipe'), may hold values from -0.125 to 0.125
- depth: float32 [2, 9, 1536], P(None, None, 'pipe'), may hold values from -2 to 2
- point: bfloat16 [2, 1536, 1536], P(None, 'pipe'), may hold values from -0.15625 to 0.15625
- bias: float32 [2, 1536], P(None, 'pipe'), may hold values from -3 to 3
- cotangent: bfloat16 [2, 128, 256, 1536], P(None, 'dp', None, 'pipe'), may hold values from -6 to 6
Outputs:
- mixed: bfloat16 [2, 128, 256, 1536], P(None, 'dp', None, 'pipe')
- grad_proj: float32 [2048, 1536], P('dp', 'pipe')
- grad_point: float32 [2, 1536, 1536], P(None, 'pipe', 'dp')
- grad_depth: float32 [2, 9, 1536], P(None, None, 'pipe')
- grad_bias: float32 [2, 1536], P(None, 'pipe')
The draws below stay inside these ranges and needn't reach their ends.
Inputs may be any that keep to these rules, and one draw needn't show every extreme that they name: In each micro-batch the counts of the 128 slides sum to 512, and the largest is exactly 16. The 16 cells of one slide in one micro-batch are distinct.
All inputs are finite; a program needn't handle non-finite values. No bound on the sum of `counts` on one device may be relied on, other than what follows from the above.
Results may differ from the reference program's by a relative error of at most 0.02.
Values may be sent and summed in bfloat16 or wider, within the bound.
No kernel may reach another device: no remote copies, remote signals or barrier semaphores. Data moves between devices by JAX's collectives and lax.ppermute only.
A program may use at most 128 MiB of HBM per device.

```python
import math
import jax
import jax.numpy as jnp
import numpy as np
from jax import lax

CH = 2048
BOT = 512
FEAT = 1536
POS = 8
TILE_DEV = 4
MB = 2
LAYERS = 2
GH = 16
GW = 16
GRID = 256
OWN = 16
SLIDES = 128
N_PIPE = 2


def draw_cells(key, part):
    key = jax.random.fold_in(key, 11)
    sub_keys = jax.random.split(key, MB * SLIDES)
    orders = jax.vmap(lambda single_key: jax.random.permutation(single_key, GRID))(sub_keys)
    return orders[:, :OWN].reshape(MB, SLIDES, OWN).astype(jnp.int32)


def block_scale(own_key, extent, cuts, smallest, largest):
    def one(position, blocks):
        draws = jax.random.uniform(jax.random.fold_in(jax.random.fold_in(own_key, 6), position), (blocks,), jnp.float32, smallest / len(cuts), largest / len(cuts))
        return jnp.repeat(jnp.exp(draws), extent[position] // blocks).reshape((-1,) + (1,) * (len(extent) - position - 1))

    loudness = one(*cuts[0])
    for cut in cuts[1:]:
        loudness = loudness * one(*cut)
    return loudness


def length_profile(count, total, reach, lean):
    portions = [(1 << 20) // math.isqrt(grade ** lean) + 1 for grade in range(2, count + 1)]
    rest, given = total - reach - (count - 1), [1] * (count - 1)
    while rest > 0:
        movable = [i for i in range(count - 1) if given[i] < reach]
        mass, left = sum([portions[i] for i in movable]), rest
        for i in movable:
            extra = min(reach - given[i], max(1, left * portions[i] // mass), rest)
            given[i] = given[i] + extra
            rest = rest - extra
    return np.array([reach] + given)


def uneven_parts(own_key, count, total, reach, skew):
    if count == 2:
        one = jax.random.randint(own_key, (), max(1, total - reach), min(reach, total - 1) + 1)
        return jnp.stack([one, total - one])
    tallies = jnp.asarray(length_profile(count, total, reach, skew), jnp.int32)
    twos = (count - 1) // 2
    source_of, receiver = tallies[1:1 + 2 * twos:2], tallies[2:2 + 2 * twos:2]
    room = jnp.minimum(source_of - 1, reach - receiver)
    passed = jax.random.randint(jax.random.fold_in(own_key, 1), (twos,), 0, 1 << 20) % (room + 1)
    tallies = tallies.at[1:1 + 2 * twos:2].set(source_of - passed).at[2:2 + 2 * twos:2].set(receiver + passed)
    return tallies[jax.random.permutation(jax.random.fold_in(own_key, 2), count)]


def gaussian(rng, shape, width, reach, cuts=(), kind=jnp.bfloat16):
    factor_of = block_scale(rng, shape, cuts, -0.22, 0.18) if cuts else 1.0
    array = jax.random.normal(rng, shape, jnp.float32) * width * factor_of
    return jnp.minimum(jnp.maximum(array, -reach), reach).astype(kind)


def setup_inputs(seed: int = 0) -> dict:
    seeds = jax.random.split(jax.random.key(seed), 11)
    return {
        "tiles": gaussian(seeds[0], (MB, SLIDES, OWN, POS, CH), 1.0, 6.0, ((1, 128),)),
        "counts": jax.vmap(lambda own: uneven_parts(own, SLIDES, TILE_DEV * SLIDES, OWN, 2))(jax.random.split(seeds[1], MB)).reshape((MB, SLIDES)).astype(jnp.int32),
        "cells": draw_cells(jax.random.fold_in(seeds[10], 71), 0),
        "block_in": gaussian(seeds[3], (N_PIPE, CH, BOT), CH ** -0.5, 0.125, ((0, 2),)),
        "block_out": gaussian(seeds[4], (N_PIPE, BOT, CH), BOT ** -0.5, 0.25, ((0, 2),)),
        "proj": gaussian(seeds[5], (CH, FEAT), CH ** -0.5, 0.125, ((1, 2),)),
        "depth": gaussian(seeds[6], (LAYERS, 9, FEAT), 9 ** -0.5, 2.0, ((2, 2),), jnp.float32),
        "point": gaussian(seeds[7], (LAYERS, FEAT, FEAT), FEAT ** -0.5, 0.15625, ((1, 2),)),
        "bias": gaussian(seeds[8], (LAYERS, FEAT), 0.5, 3.0, ((1, 2),), jnp.float32),
        "cotangent": gaussian(seeds[9], (MB, SLIDES, GRID, FEAT), 1.0, 6.0, ((1, 128), (3, 2))),
    }


def encode_block(row_block, w_in, w_out):
    hidden = jnp.maximum(jnp.dot(row_block, w_in, preferred_element_type=jnp.float32), 0.0).astype(jnp.bfloat16)
    summed = row_block.astype(jnp.float32) + jnp.dot(hidden, w_out, preferred_element_type=jnp.float32)
    return jnp.maximum(summed, 0.0).astype(jnp.bfloat16)

def dilated(field_f, kernel, dilation):
    height, breadth = (field_f.shape[1], field_f.shape[2])
    padded = jnp.pad(field_f, ((0, 0), (dilation, dilation), (dilation, dilation), (0, 0)))
    result = jnp.zeros_like(field_f)
    for row_off in range(3):
        for col_off in range(3):
            taps = padded[:, row_off * dilation:row_off * dilation + height, col_off * dilation:col_off * dilation + breadth, :]
            result = result + taps * kernel[3 * row_off + col_off]
    return result

def dilated_back(field_f, kernel, grad_out, dilation):
    height, breadth = (field_f.shape[1], field_f.shape[2])
    widths = ((0, 0), (dilation, dilation), (dilation, dilation), (0, 0))
    padded_field = jnp.pad(field_f, widths)
    padded_grad = jnp.pad(grad_out, widths)
    field_grad = jnp.zeros_like(field_f)
    kernel_rows = []
    for row_off in range(3):
        for col_off in range(3):
            taps = padded_field[:, row_off * dilation:row_off * dilation + height, col_off * dilation:col_off * dilation + breadth, :]
            kernel_rows.append(lax.optimization_barrier(jnp.sum(taps * grad_out, axis=(0, 1, 2))))
            back_row = (2 - row_off) * dilation
            back_col = (2 - col_off) * dilation
            field_grad = field_grad + padded_grad[:, back_row:back_row + height, back_col:back_col + breadth, :] * kernel[3 * row_off + col_off]
    return (field_grad, jnp.stack(kernel_rows))

def reference(tiles, counts, cells, block_in, block_out, proj, depth, point, bias, cotangent):
    slot_ids = jnp.arange(OWN, dtype=jnp.int32)
    pooled_list = []
    target_list = []
    grid_list = []
    occupied_list = []
    for micro_id in range(MB):
        is_live = (slot_ids[None, :] < counts[micro_id][:, None]).reshape(-1)
        live_index = jnp.nonzero(is_live, size=TILE_DEV * SLIDES)[0].astype(jnp.int32)
        packed = tiles[micro_id].reshape(SLIDES * OWN, POS, CH)[live_index]
        row_block = packed.reshape(-1, CH)
        for section in range(N_PIPE):
            row_block = encode_block(row_block, block_in[section], block_out[section])
        pooled = (lax.optimization_barrier(jnp.sum(row_block.reshape(-1, POS, CH).astype(jnp.float32), axis=1)) / POS).astype(jnp.bfloat16)
        features = jnp.dot(pooled, proj, preferred_element_type=jnp.float32).astype(jnp.bfloat16)
        target = (live_index // OWN).astype(jnp.int32) * GRID + cells[micro_id].reshape(-1)[live_index].astype(jnp.int32)
        grid_list.append(jnp.zeros((SLIDES * GRID, FEAT), jnp.bfloat16).at[target].set(features))
        occupied_list.append(jnp.zeros((SLIDES * GRID,), jnp.float32).at[target].set(1.0))
        pooled_list.append(pooled)
        target_list.append(target)
    cell_grid = jnp.concatenate(grid_list, axis=0)
    occupied = jnp.concatenate(occupied_list, axis=0)[:, None]
    batch = MB * SLIDES
    saved = []
    for layer_id in range(LAYERS):
        dilation = 2 ** (layer_id + 1)
        field_f = cell_grid.astype(jnp.float32).reshape(batch, GH, GW, FEAT)
        spread_u = dilated(field_f, depth[layer_id], dilation).reshape(-1, FEAT).astype(jnp.bfloat16)
        pre_act = jnp.dot(spread_u, point[layer_id], preferred_element_type=jnp.float32) + bias[layer_id]
        saved.append((cell_grid, spread_u, pre_act))
        cell_grid = ((cell_grid.astype(jnp.float32) + jax.nn.gelu(pre_act)) * occupied).astype(jnp.bfloat16)
    mixed = cell_grid.reshape(MB, SLIDES, GRID, FEAT)
    upstream = cotangent.astype(jnp.float32).reshape(-1, FEAT)
    point_grads = [None] * LAYERS
    depth_grads = [None] * LAYERS
    bias_grads = [None] * LAYERS
    for layer_id in reversed(range(LAYERS)):
        dilation = 2 ** (layer_id + 1)
        grid_in, spread_u, pre_act = saved[layer_id]
        masked = upstream * occupied
        slope_grad = jax.vjp(jax.nn.gelu, pre_act)[1](masked)[0]
        bias_grads[layer_id] = lax.optimization_barrier(jnp.sum(slope_grad, axis=0))
        slope_half = slope_grad.astype(jnp.bfloat16)
        point_grads[layer_id] = jnp.dot(spread_u.T, slope_half, preferred_element_type=jnp.float32)
        spread_grad = jnp.dot(slope_half, point[layer_id].T, preferred_element_type=jnp.float32)
        field_grad, depth_grad = dilated_back(grid_in.astype(jnp.float32).reshape(batch, GH, GW, FEAT), depth[layer_id], spread_grad.reshape(batch, GH, GW, FEAT), dilation)
        depth_grads[layer_id] = depth_grad
        upstream = masked + field_grad.reshape(-1, FEAT)
    per_micro = upstream.reshape(MB, SLIDES * GRID, FEAT)
    proj_grad = jnp.zeros((CH, FEAT), jnp.float32)
    for micro_id in range(MB):
        tile_grad = per_micro[micro_id][target_list[micro_id]].astype(jnp.bfloat16)
        proj_grad = proj_grad + jnp.dot(pooled_list[micro_id].T, tile_grad, preferred_element_type=jnp.float32)
    return (mixed, proj_grad, jnp.stack(point_grads), jnp.stack(depth_grads), jnp.stack(bias_grads))
```

```python
import jax
import jax.numpy as jnp
from jax import lax
from jax.experimental import pallas as pl
from jax.experimental.pallas import tpu as pltpu
from jax.sharding import Mesh, PartitionSpec as P

MB = 2
OWN = 16
POS = 8
ROWS = MB * OWN
CH = 2048
FEAT = 1536
HALF = 768
CELLS = 256
NZ, NY, NX = 8, 4, 4
PLANE = NY * NX
COLS = 12
BF = jnp.bfloat16
F32 = jnp.float32
VM = pl.BlockSpec(memory_space=pltpu.VMEM)
SM = pl.BlockSpec(memory_space=pltpu.SMEM)
PARAMS = pltpu.CompilerParams(vmem_limit_bytes=48 * 1024 * 1024)
TG, SP, SL, DG = 0, 32, 96, 112
MSG = 144


def dot(a, b):
    return jnp.dot(a, b, preferred_element_type=F32)


def iota(shape, axis):
    return lax.broadcasted_iota(jnp.int32, shape, axis)


def slot_maps(cells_ref, counts_ref):
    rows, cols = iota((ROWS, ROWS), 0), iota((ROWS, ROWS), 1)
    cell_r = jnp.zeros((ROWS, ROWS), jnp.int32)
    cell_c = jnp.zeros((ROWS, ROWS), jnp.int32)
    for m in range(MB):
        for j in range(OWN):
            cell = cells_ref[m, 0, j]
            cell_r = jnp.where(rows == m * OWN + j, cell, cell_r)
            cell_c = jnp.where(cols == m * OWN + j, cell, cell_c)
    live_r = (rows & (OWN - 1)) < jnp.where(rows < OWN, counts_ref[0, 0], counts_ref[1, 0])
    live_c = (cols & (OWN - 1)) < jnp.where(cols < OWN, counts_ref[0, 0], counts_ref[1, 0])
    pair = live_r & live_c & ((rows >> 4) == (cols >> 4))
    down = (cell_c >> 4) - (cell_r >> 4)
    right = (cell_c & 15) - (cell_r & 15)
    return pair, down, right


def tap_matrix(maps, dilation):
    pair, down, right = maps
    taps = []
    for a in range(3):
        for b in range(3):
            hit = pair & (down == (a - 1) * dilation) & (right == (b - 1) * dilation)
            taps.append(jnp.where(hit, 1.0, 0.0))
    return jnp.concatenate(taps, axis=0).astype(BF)


def live_rows(counts_ref, width):
    rows = iota((ROWS, width), 0)
    return (rows & (OWN - 1)) < jnp.where(rows < OWN, counts_ref[0, 0], counts_ref[1, 0])


def placed(cells_ref, counts_ref, m):
    rows, cols = iota((OWN, CELLS), 0), iota((OWN, CELLS), 1)
    cell = jnp.zeros((OWN, CELLS), jnp.int32)
    for j in range(OWN):
        cell = jnp.where(rows == j, cells_ref[m, 0, j], cell)
    return jnp.where((cell == cols) & (rows < counts_ref[m, 0]), 1.0, 0.0)


def weighted(shifted, depth_ref, layer, backward=False):
    total = None
    for t in range(9):
        s = 8 - t if backward else t
        term = shifted[s * ROWS : (s + 1) * ROWS] * depth_ref[layer, t : t + 1, :]
        total = term if total is None else total + term
    return total


def gelu_parts(x):
    c = 0.7978845608028654
    t = jnp.tanh(c * (x + 0.044715 * (x * x * x)))
    half = 0.5 * (1.0 + t)
    slope = half + 0.5 * x * (1.0 - t * t) * (c * (1.0 + 3 * 0.044715 * (x * x)))
    return x * half, slope


def whole(p_ref, own, other):
    first = p_ref[0] == 0
    return jnp.concatenate([jnp.where(first, own, other), jnp.where(first, other, own)], axis=1)


def encode(x_ref, w_in_ref, w_out_ref):
    x = x_ref[...]
    hidden = jnp.maximum(dot(x, w_in_ref[0]), 0.0).astype(BF)
    return jnp.maximum(x.astype(F32) + dot(hidden, w_out_ref[0]), 0.0).astype(BF)


def first_section(x_ref, w_in_ref, w_out_ref, out_ref):
    out_ref[...] = encode(x_ref, w_in_ref, w_out_ref)


def second_section(x_ref, w_in_ref, w_out_ref, out_ref):
    n = ROWS * POS
    pool = jnp.where(iota((ROWS, n), 1) >> 3 == iota((ROWS, n), 0), 1.0 / POS, 0.0).astype(BF)
    out_ref[...] = dot(pool, encode(x_ref, w_in_ref, w_out_ref)).astype(BF)


def enter(p_ref, cells_ref, counts_ref, mine_ref, got_ref, proj_ref, depth_ref, point_ref,
          bias_ref, cot_ref, pooled_ref, feat_ref, spread_ref, part_ref, msg_ref):
    pooled = jnp.where(p_ref[0] == 1, mine_ref[...], got_ref[...])
    pooled_ref[...] = pooled
    feat = jnp.where(live_rows(counts_ref, HALF), dot(pooled, proj_ref[...]), 0.0).astype(BF)
    feat_ref[...] = feat
    maps = slot_maps(cells_ref, counts_ref)
    spread = weighted(dot(tap_matrix(maps, 2), feat), depth_ref, 0).astype(BF)
    spread_ref[...] = spread
    left = dot(spread, point_ref[0, :, :HALF])
    right = dot(spread, point_ref[0, :, HALF:])
    first = p_ref[0] == 0
    part_ref[...] = jnp.where(first, left, right)
    msg_ref[:ROWS] = jnp.where(first, right, left)
    for m in range(MB):
        rows = dot(placed(cells_ref, counts_ref, m).astype(BF), cot_ref[m, 0])
        msg_ref[ROWS + m * OWN : ROWS + (m + 1) * OWN] = rows
    msg_ref[2 * ROWS :] = jnp.broadcast_to(bias_ref[1:2], (8, HALF))


def second_layer(cells_ref, counts_ref, part_ref, got_ref, feat_ref, bias_ref, depth_ref,
                 point_ref, pre_ref, grid_ref, spread_ref, mix_ref):
    pre = part_ref[...] + got_ref[:ROWS] + bias_ref[0:1]
    pre_ref[...] = pre
    value = feat_ref[...].astype(F32) + gelu_parts(pre)[0]
    grid = jnp.where(live_rows(counts_ref, HALF), value, 0.0).astype(BF)
    grid_ref[...] = grid
    maps = slot_maps(cells_ref, counts_ref)
    spread = weighted(dot(tap_matrix(maps, 4), grid), depth_ref, 1).astype(BF)
    spread_ref[...] = spread
    mix_ref[...] = dot(spread, point_ref[0])


def split_taps(taps, value):
    high = value.astype(BF)
    low = (value - high.astype(F32)).astype(BF)
    return dot(taps, high) + dot(taps, low)


def turn(p_ref, cells_ref, counts_ref, mix_ref, got_mix_ref, msg_ref, got_ref, pre_ref, grid_ref,
         depth_ref, point_ref, mixed_ref, slope1_ref, slope0_ref, masked_ref, grads_ref):
    cot = msg_ref[ROWS : 2 * ROWS]
    cot_all = whole(p_ref, cot, got_ref[ROWS : 2 * ROWS])
    bias_all = whole(p_ref, msg_ref[2 * ROWS :], got_ref[2 * ROWS :])[0:1]
    pre = mix_ref[...] + got_mix_ref[...] + bias_all
    value, deriv = gelu_parts(pre)
    slope = cot_all * deriv
    slope_half = slope.astype(BF)
    slope1_ref[...] = slope_half
    first = p_ref[0] == 0
    value = jnp.where(first, value[:, :HALF], value[:, HALF:])
    slope = jnp.where(first, slope[:, :HALF], slope[:, HALF:])
    grid = grid_ref[...]
    live = live_rows(counts_ref, HALF)
    mixed = jnp.where(live, grid.astype(F32) + value, 0.0).astype(BF)
    for m in range(MB):
        mixed_ref[m, 0] = lax.dot_general(
            placed(cells_ref, counts_ref, m).astype(BF), mixed[m * OWN : (m + 1) * OWN],
            (((0,), (0,)), ((), ())), preferred_element_type=F32).astype(BF)
    spread_grad = lax.dot_general(slope_half, point_ref[0], (((1,), (1,)), ((), ())),
                                  preferred_element_type=F32)
    taps = tap_matrix(slot_maps(cells_ref, counts_ref), 4)
    field = dot(taps, grid)
    rows = iota((16, HALF), 0)
    grads = jnp.where(rows == 9, jnp.sum(slope, axis=0, keepdims=True), 0.0)
    for t in range(9):
        row = jnp.sum(field[t * ROWS : (t + 1) * ROWS] * spread_grad, axis=0, keepdims=True)
        grads = jnp.where(rows == t, row, grads)
    back = weighted(split_taps(taps, spread_grad), depth_ref, 1, backward=True)
    masked = jnp.where(live, cot + back, 0.0)
    masked_ref[...] = masked
    slope0 = masked * gelu_parts(pre_ref[...])[1]
    slope0_ref[...] = slope0.astype(BF)
    grads_ref[...] = jnp.where(rows == 10, jnp.sum(slope0, axis=0, keepdims=True), grads)


def column_picker(depth, step, keep):
    rows, cols = iota((2 * depth, PLANE * 128), 0), iota((2 * depth, PLANE * 128), 1)
    row = iota((2 * depth, 1), 0)
    second = row >= depth
    rest = jnp.where(second, row - depth, row)
    group = jnp.zeros_like(rest)
    for g in range(1, PLANE):
        group = group + jnp.where(rest >= g * keep, 1, 0)
    target = group * 128 + (rest - group * keep) + jnp.where(second, step, 0)
    del rows
    return jnp.where(cols == target, 1.0, 0.0).astype(BF)


def picked(value, depth, keep):
    count = value.shape[0]
    parts = [value[:, 2 * depth * i : 2 * depth * (i + 1)] for i in range(4)]
    spread = dot(jnp.concatenate(parts, axis=0), column_picker(depth, 16, keep))
    out = []
    for g in range(PLANE):
        total = spread[:count, g * 128 : (g + 1) * 128]
        for i in range(1, 4):
            piece = spread[i * count : (i + 1) * count, g * 128 : (g + 1) * 128]
            total = total + pltpu.roll(piece, 32 * i, 1)
        out.append(total.astype(BF))
    return out


def leave(p_ref, cells_ref, counts_ref, slope0_ref, got_ref, slope1_ref, feat_ref, spread0_ref,
          spread1_ref, depth_ref, point_ref, masked_ref, grads_ref, pooled_ref, out_ref):
    slope0 = whole(p_ref, slope0_ref[...], got_ref[...])
    spread_grad = lax.dot_general(slope0, point_ref[0], (((1,), (1,)), ((), ())),
                                  preferred_element_type=F32)
    taps = tap_matrix(slot_maps(cells_ref, counts_ref), 2)
    field = dot(taps, feat_ref[...])
    rows = iota((32, HALF), 0)
    grads = jnp.concatenate([grads_ref[...], jnp.zeros((16, HALF), F32)], axis=0)
    for t in range(9):
        row = jnp.sum(field[t * ROWS : (t + 1) * ROWS] * spread_grad, axis=0, keepdims=True)
        grads = jnp.where(rows == (11 + t if t < 5 else 23 + t), row, grads)
    grads = grads.astype(BF)
    back = weighted(split_taps(taps, spread_grad), depth_ref, 0, backward=True)
    tile_grad = jnp.where(live_rows(counts_ref, HALF), masked_ref[...] + back, 0.0).astype(BF)
    slopes = picked(jnp.concatenate([slope0, slope1_ref[...]], axis=0), 192, COLS)
    pooled = picked(pooled_ref[...], 256, 16)
    for g in range(PLANE):
        out_ref[g, TG : TG + ROWS] = tile_grad
        out_ref[g, SP : SP + ROWS] = spread0_ref[...]
        out_ref[g, SP + ROWS : SP + 2 * ROWS] = spread1_ref[...]
        for side in range(2):
            r = slice(16 * side, 16 * side + 16)
            at = 384 * side
            out_ref[g, SL : SL + 16, at : at + 128] = slopes[g][r]
            out_ref[g, SL : SL + 16, at + 128 : at + 256] = slopes[g][32 + 16 * side : 48 + 16 * side]
            out_ref[g, SL : SL + 16, at + 256 : at + 384] = pooled[g][r]
        out_ref[g, DG : DG + 32] = grads


def products(in_ref, out_ref):
    n = PLANE * ROWS

    def rows_at(start):
        return in_ref[:, start : start + ROWS, :].reshape(n, HALF)

    def cols_at(lane):
        parts = [in_ref[:, SL : SL + 16, lane + 384 * s : lane + 384 * s + 128] for s in range(2)]
        return jnp.concatenate(parts, axis=1).reshape(n, 128)

    def outer(a, b):
        return lax.dot_general(a, b, (((0,), (0,)), ((), ())), preferred_element_type=F32)

    point0 = outer(cols_at(0), rows_at(SP))
    point1 = outer(cols_at(128), rows_at(SP + ROWS))
    proj = outer(cols_at(256), rows_at(TG))
    grads = in_ref[0, DG : DG + 32, :].astype(F32)
    for g in range(1, PLANE):
        grads = grads + in_ref[g, DG : DG + 32, :].astype(F32)
    for z in range(NZ):
        r = slice(16 * z, 16 * z + 16)
        out_ref[z, 0:16] = (point0[r] + grads[16:32]).astype(BF)
        out_ref[z, 16:32] = point1[r].astype(BF)
        out_ref[z, 32:48] = proj[r].astype(BF)
        out_ref[z, 48:64] = grads[0:16].astype(BF)


def finish(in_ref, proj_ref, point_ref, depth_ref, bias_ref):
    total = in_ref[0].astype(F32)
    for z in range(1, NZ):
        total = total + in_ref[z].astype(F32)
    proj_ref[...] = total[32:48]
    for layer in range(2):
        point_ref[layer] = total[16 * layer : 16 * layer + 16].T[:, :COLS]
    depth_ref[1] = total[48:57]
    bias_ref[1:2] = total[57:58]
    bias_ref[0:1] = total[58:59]
    depth_ref[0, 0:5] = total[59:64]
    depth_ref[0, 5:9] = total[12:16]


def call(body, outs, specs, *args):
    return pl.pallas_call(
        body, out_shape=[jax.ShapeDtypeStruct(s, d) for s, d in outs], in_specs=specs, grid=(1,),
        out_specs=[VM] * len(outs), compiler_params=PARAMS, name=body.__name__)(*args)


def layer_of(i):
    return pl.BlockSpec((1, HALF, FEAT), lambda _: (i, 0, 0))


def swap(value):
    return lax.ppermute(value, "pipe", [(0, 1), (1, 0)])


def shards(tiles, counts, cells, block_in, block_out, proj, depth, point, bias, cotangent):
    p = lax.axis_index("pipe").astype(jnp.int32).reshape(1)
    x = tiles.reshape(ROWS * POS, CH)
    (x,) = call(first_section, [(x.shape, BF)], [VM] * 3, x, block_in, block_out)
    x = lax.ppermute(x, "pipe", [(0, 1)])
    (mine,) = call(second_section, [((ROWS, CH), BF)], [VM] * 3, x, block_in, block_out)
    got = lax.ppermute(mine, "pipe", [(1, 0)])
    half_b, half_f = ((ROWS, HALF), BF), ((ROWS, HALF), F32)
    pooled, feat, spread0, part, msg = call(
        enter, [((ROWS, CH), BF), half_b, half_b, half_f, ((2 * ROWS + 8, HALF), F32)],
        [SM, SM, SM, VM, VM, VM, VM, layer_of(0), VM, VM],
        p, cells, counts, mine, got, proj, depth, point, bias, cotangent)
    got_msg = swap(msg)
    pre0, grid1, spread1, mix = call(
        second_layer, [half_f, half_b, half_b, ((ROWS, FEAT), F32)],
        [SM, SM, VM, VM, VM, VM, VM, layer_of(1)],
        cells, counts, part, got_msg, feat, bias, depth, point)
    got_mix = swap(mix)
    mixed, slope1, slope0, masked, grads = call(
        turn, [((MB, 1, CELLS, HALF), BF), ((ROWS, FEAT), BF), half_b, half_f, ((16, HALF), F32)],
        [SM, SM, SM] + [VM] * 7 + [layer_of(1)],
        p, cells, counts, mix, got_mix, msg, got_msg, pre0, grid1, depth, point)
    got_slope = swap(slope0)
    (rows,) = call(
        leave, [((PLANE, MSG, HALF), BF)],
        [SM, SM, SM] + [VM] * 7 + [layer_of(0)] + [VM] * 3,
        p, cells, counts, slope0, got_slope, slope1, feat, spread0, spread1, depth, point, masked,
        grads, pooled)
    rows = lax.all_to_all(rows, ("y", "x"), 0, 0, tiled=True)
    (sums,) = call(products, [((NZ, 64, HALF), BF)], [VM], rows)
    sums = lax.all_to_all(sums, "z", 0, 0, tiled=True)
    grad_proj, grad_point, grad_depth, grad_bias = call(
        finish, [((16, HALF), F32), ((2, HALF, COLS), F32), ((2, 9, HALF), F32), ((2, HALF), F32)],
        [VM], sums)
    return mixed, grad_proj, grad_point, grad_depth, grad_bias


def solution(mesh):
    grid = Mesh(mesh.devices.reshape(2, NZ, NY, NX), ("pipe", "z", "y", "x"))
    dp = ("z", "y", "x")
    in_specs = (
        P(None, dp, None, None, None),
        P(None, dp),
        P(None, dp, None),
        P("pipe", None, None),
        P("pipe", None, None),
        P(None, "pipe"),
        P(None, None, "pipe"),
        P(None, "pipe", None),
        P(None, "pipe"),
        P(None, dp, None, "pipe"),
    )
    out_specs = (
        P(None, dp, None, "pipe"),
        P(dp, "pipe"),
        P(None, "pipe", dp),
        P(None, None, "pipe"),
        P(None, "pipe"),
    )
    return jax.shard_map(shards, mesh=grid, in_specs=in_specs, out_specs=out_specs, check_vma=False)
```

```python
import jax
import jax.numpy as jnp
from jax import lax
from jax.experimental import pallas as pl
from jax.experimental.pallas import tpu as pltpu
from jax.sharding import Mesh, PartitionSpec as P

MB = 2
OWN = 16
POS = 8
ROWS = MB * OWN
CH = 2048
FEAT = 1536
HALF = 768
CELLS = 256
NZ, NY, NX = 8, 4, 4
PLANE = NY * NX
ALL = NZ * ROWS
SLICE = CH // NZ
COLS = 12
WIDTH = HALF + SLICE
SIDE = HALF + 128
STEP = 16
BF = jnp.bfloat16
F32 = jnp.float32
VM = pl.BlockSpec(memory_space=pltpu.VMEM)
HB = pl.BlockSpec(memory_space=pltpu.HBM)
SM = pl.BlockSpec(memory_space=pltpu.SMEM)


def dot(a, b):
    return jnp.dot(a, b, preferred_element_type=F32)


def dot_nt(a, b):
    return lax.dot_general(a, b, (((1,), (1,)), ((), ())), preferred_element_type=F32)


def dot_tn(a, b):
    return lax.dot_general(a, b, (((0,), (0,)), ((), ())), preferred_element_type=F32)


def iota(shape, axis):
    return lax.broadcasted_iota(jnp.int32, shape, axis)


def halves():
    p = lax.axis_index("pipe")
    mine = pl.multiple_of(p * HALF, 128)
    other = pl.multiple_of((1 - p) * HALF, 128)
    return pl.ds(mine, HALF), pl.ds(other, HALF)


def own_live(counts_ref, width):
    rows = iota((ROWS, width), 0)
    return (rows & (OWN - 1)) < jnp.where(rows < OWN, counts_ref[0, 0], counts_ref[1, 0])


def wide(code, times):
    return jnp.concatenate([code.astype(F32)] * times, axis=1)


def live_at(side_ref, rows):
    return wide(side_ref[rows, HALF:], HALF // 128) >= 0


def taps(side_ref, near_ref, near_long_ref, far_ref, far_long_ref):
    code = wide(side_ref[:, HALF:], 2)
    rows, cols = code.astype(jnp.int32), code.T.astype(jnp.int32)
    block = (iota((ALL, ALL), 0) >> 4) == (iota((ALL, ALL), 1) >> 4)
    pair = block & (rows >= 0) & (cols >= 0)
    down = jnp.where(pair, (cols >> 4) - (rows >> 4), 64)
    right = (cols & 15) - (rows & 15)
    for dilation, out_ref, long_ref in ((2, near_ref, near_long_ref), (4, far_ref, far_long_ref)):
        for t in range(9):
            hit = (down == (t // 3 - 1) * dilation) & (right == (t % 3 - 1) * dilation)
            hit = jnp.where(hit, 1.0, 0.0).astype(BF)
            out_ref[:, t * ALL : (t + 1) * ALL] = hit
            long_ref[t * ALL : (t + 1) * ALL] = hit


def chunks():
    return [slice(i, i + STEP) for i in range(0, ALL, STEP)]


def put_weighed(stack, rows, value, depth_ref, layer, backward):
    for t in range(9):
        s = 8 - t if backward else t
        at = slice(t * ALL + rows.start, t * ALL + rows.stop)
        stack[at] = (value * depth_ref[s, layer : layer + 1, :]).astype(BF)


def depth_rows(long_ref, grid, grad, moved, out_ref, rows):
    moved[...] = dot(long_ref[...], grid)
    for at in (slice(0, 384), slice(384, HALF)):
        sums = [None] * 9
        for i in range(0, ALL, 8):
            value = grad[i : i + 8, at]
            for t in range(9):
                term = moved[t * ALL + i : t * ALL + i + 8, at] * value
                sums[t] = term if sums[t] is None else sums[t] + term
        for t in range(9):
            out_ref[rows[t] : rows[t] + 1, at] = jnp.sum(sums[t], axis=0, keepdims=True)


def gelu_parts(x):
    c = 0.7978845608028654
    t = jnp.tanh(c * (x + 0.044715 * (x * x * x)))
    half = 0.5 * (1.0 + t)
    slope = half + 0.5 * x * (1.0 - t * t) * (c * (1.0 + 3 * 0.044715 * (x * x)))
    return x * half, slope


def encode(x_ref, w_in_ref, w_out_ref):
    x = x_ref[...]
    hidden = jnp.maximum(dot(x, w_in_ref[0]), 0.0).astype(BF)
    return jnp.maximum(x.astype(F32) + dot(hidden, w_out_ref[0]), 0.0).astype(BF)


def first_section(x_hbm, w_in_hbm, w_out_hbm, out_ref, x_ref, w_in_ref, w_out_ref, sems):
    n = 4
    step = CH // n
    copies = []
    for k in range(n):
        at = pl.ds(k * step, step)
        copies.append(pltpu.make_async_copy(x_hbm.at[:, at], x_ref.at[:, at], sems.at[0, k]))
        copies.append(pltpu.make_async_copy(w_in_hbm.at[0, at], w_in_ref.at[at], sems.at[1, k]))
    for k in range(n):
        at = pl.ds(k * step, step)
        copies.append(pltpu.make_async_copy(w_out_hbm.at[0, :, at], w_out_ref.at[:, at], sems.at[2, k]))
    for copy in copies:
        copy.start()
    hidden = None
    for k in range(n):
        at = slice(k * step, (k + 1) * step)
        copies[2 * k].wait()
        copies[2 * k + 1].wait()
        part = dot(x_ref[:, at], w_in_ref[at])
        hidden = part if hidden is None else hidden + part
    hidden = jnp.maximum(hidden, 0.0).astype(BF)
    for k in range(n):
        at = slice(k * step, (k + 1) * step)
        copies[2 * n + k].wait()
        total = x_ref[:, at].astype(F32) + dot(hidden, w_out_ref[:, at])
        out_ref[:, at] = jnp.maximum(total, 0.0).astype(BF)


def second_section(x_ref, w_in_hbm, w_out_hbm, out_ref, w_in_ref, w_out_ref, sems):
    n = ROWS * POS
    ins, outs = [], []
    for k in range(2):
        at = pl.ds(k * (CH // 2), CH // 2)
        ins.append(pltpu.make_async_copy(w_in_hbm.at[0, at], w_in_ref.at[at], sems.at[0, k]))
        outs.append(
            pltpu.make_async_copy(w_out_hbm.at[0, :, at], w_out_ref.at[:, at], sems.at[1, k]))
    for copy in ins + outs:
        copy.start()
    pool = jnp.where(iota((ROWS, n), 1) >> 3 == iota((ROWS, n), 0), 1.0 / POS, 0.0).astype(BF)
    hidden = None
    for k in range(2):
        at = slice(k * (CH // 2), (k + 1) * (CH // 2))
        ins[k].wait()
        part = dot(x_ref[:, at], w_in_ref[at])
        hidden = part if hidden is None else hidden + part
    hidden = jnp.maximum(hidden, 0.0).astype(BF)
    for k in range(2):
        at = slice(k * (CH // 2), (k + 1) * (CH // 2))
        outs[k].wait()
        total = x_ref[:, at].astype(F32) + dot(hidden, w_out_ref[:, at])
        out_ref[:, at] = dot(pool, jnp.maximum(total, 0.0).astype(BF)).astype(BF)


def side_rows(cells_ref, counts_ref, cot_ref, out_ref):
    rows = iota((ROWS, 128), 0)
    code = jnp.zeros((ROWS, 128), jnp.int32)
    for m in range(MB):
        for j in range(OWN):
            code = jnp.where(rows == m * OWN + j, cells_ref[m, 0, j], code)
    code = jnp.where(own_live(counts_ref, 128), code, -1)
    double = jnp.concatenate([code, code], axis=1)
    code = code.astype(F32).astype(BF)
    hit = jnp.where(double == iota((ROWS, CELLS), 1), 1.0, 0.0).astype(BF)
    for m in range(MB):
        at = slice(m * OWN, (m + 1) * OWN)
        cot = dot(hit[at], cot_ref[m, 0]).astype(BF)
        for z in range(NZ):
            out_ref[z, at, :HALF] = cot
            out_ref[z, at, HALF:] = code[at]


def project(side_ref, mine_ref, got_ref, proj_ref, out_ref):
    pooled = jnp.where(lax.axis_index("pipe") == 1, mine_ref[...], got_ref[...])
    live = wide(side_ref[0, :, HALF:], HALF // 128) >= 0
    feat = jnp.where(live, dot(pooled, proj_ref[...]), 0.0).astype(BF)
    for z in range(NZ):
        out_ref[z, :, :HALF] = feat
        out_ref[z, :, HALF:] = pooled[:, z * SLICE : (z + 1) * SLICE]


def mix(spread_ref, w, part_ref, send_ref):
    mine, other = halves()
    send_ref[...] = dot(spread_ref[...], w[:, other]).astype(BF)
    part_ref[...] = dot(spread_ref[...], w[:, mine])


def unmix(slope_ref, got_ref, point_ref, layer):
    mine, other = halves()
    own = dot_nt(slope_ref[...], point_ref[layer, :, mine])
    return own + dot_nt(got_ref[...], point_ref[layer, :, other])


def layer0(slots_ref, depth_ref, near_ref, point_ref, spread_ref, part_ref, send_ref,
           stack, w, sem):
    copy = pltpu.make_async_copy(point_ref.at[0], w, sem)
    copy.start()
    for rows in chunks():
        put_weighed(stack, rows, slots_ref[rows, :HALF].astype(F32), depth_ref, 0, False)
    spread_ref[...] = dot(near_ref[...], stack[...]).astype(BF)
    copy.wait()
    mix(spread_ref, w, part_ref, send_ref)


def layer1(slots_ref, side_ref, part_ref, got_ref, depth_ref, bias_ref, far_ref, point_ref,
           pre_ref, grid_ref, spread_ref, part_out_ref, send_ref, stack, w, sem):
    copy = pltpu.make_async_copy(point_ref.at[1], w, sem)
    copy.start()
    for rows in chunks():
        pre = part_ref[rows] + got_ref[rows].astype(F32) + bias_ref[0:1]
        pre_ref[rows] = pre
        value = slots_ref[rows, :HALF].astype(F32) + gelu_parts(pre)[0]
        grid = jnp.where(live_at(side_ref, rows), value, 0.0).astype(BF)
        grid_ref[rows] = grid
        put_weighed(stack, rows, grid.astype(F32), depth_ref, 1, False)
    spread_ref[...] = dot(far_ref[...], stack[...]).astype(BF)
    copy.wait()
    mix(spread_ref, w, part_out_ref, send_ref)


def head(side_ref, part_ref, got_ref, grid_ref, bias_ref,
         mixed_ref, slope_ref, sum_ref, mixed, sem):
    for m in range(MB):
        at = pl.ds(pl.multiple_of(lax.axis_index("z") * ROWS + m * OWN, OWN), OWN)
        pre = part_ref[at] + got_ref[at].astype(F32) + bias_ref[1:2]
        rows = (grid_ref[at].astype(F32) + gelu_parts(pre)[0]).astype(BF)
        code = wide(side_ref[at, HALF:], 2).astype(jnp.int32)
        hit = jnp.where(code == iota((OWN, CELLS), 1), 1.0, 0.0).astype(BF)
        mixed[m, 0] = dot_tn(hit, rows).astype(BF)
    out = pltpu.make_async_copy(mixed, mixed_ref, sem)
    out.start()
    total = None
    for rows in chunks():
        pre = part_ref[rows] + got_ref[rows].astype(F32) + bias_ref[1:2]
        slope = side_ref[rows, :HALF].astype(F32) * gelu_parts(pre)[1]
        slope = jnp.where(live_at(side_ref, rows), slope, 0.0)
        slope_ref[rows] = slope.astype(BF)
        total = slope if total is None else total + slope
    sum_ref[...] = jnp.sum(total, axis=0, keepdims=True)
    out.wait()


def back1(side_ref, slope_ref, got_ref, grid_ref, pre_ref, sum_ref, depth_ref, far_ref,
          far_long_ref, point_ref, masked_ref, out_ref, grads_ref, stack, moved, grad):
    grad[...] = unmix(slope_ref, got_ref, point_ref, 1)
    for rows in chunks():
        put_weighed(stack, rows, grad[rows], depth_ref, 1, True)
    grads_ref[...] = jnp.zeros((16, HALF), F32)
    depth_rows(far_long_ref, grid_ref[...], grad, moved, grads_ref, list(range(9)))
    grad[...] = dot(far_ref[...], stack[...])
    total = None
    for rows in chunks():
        masked = side_ref[rows, :HALF].astype(F32) + grad[rows]
        masked = jnp.where(live_at(side_ref, rows), masked, 0.0)
        masked_ref[rows] = masked
        slope = masked * gelu_parts(pre_ref[rows])[1]
        out_ref[rows] = slope.astype(BF)
        total = slope if total is None else total + slope
    grads_ref[9:10] = sum_ref[...]
    grads_ref[10:11] = jnp.sum(total, axis=0, keepdims=True)


def slope_rows(side, values):
    row = iota((256, 1), 0)
    group, i = row >> 4, row & 15
    column = lax.axis_index("z") * 192 + group * COLS + i - side * HALF
    column = jnp.where(i < COLS, column, -1)
    picker = jnp.where(iota((256, HALF), 1) == column, 1.0, 0.0).astype(BF)
    return [dot_nt(picker, value) for value in values]


def back0(slots_ref, side_ref, slope_ref, got_ref, slope1_ref, got1_ref, spread0_ref, spread1_ref,
          masked_ref, grads_ref, depth_ref, near_ref, near_long_ref, point_ref, out_ref,
          stack, moved, grad, grads):
    p = lax.axis_index("pipe")
    own = slope_rows(p, (slope_ref[...], slope1_ref[...]))
    far = slope_rows(1 - p, (got_ref[...], got1_ref[...]))
    point0 = dot((own[0] + far[0]).astype(BF), spread0_ref[...])
    point1 = dot((own[1] + far[1]).astype(BF), spread1_ref[...]).astype(BF)
    for g in range(PLANE):
        out_ref[g, 16:32] = point1[16 * g : 16 * g + 16]
    grad[...] = unmix(slope_ref, got_ref, point_ref, 0)
    for rows in chunks():
        put_weighed(stack, rows, grad[rows], depth_ref, 0, True)
    grads[0:16] = grads_ref[...]
    grads[16:32] = jnp.zeros((16, HALF), F32)
    where = [11 + t if t < 5 else 23 + t for t in range(9)]
    depth_rows(near_long_ref, slots_ref[:, :HALF], grad, moved, grads, where)
    tail, last = grads[16:32], grads[0:16].astype(BF)
    for g in range(PLANE):
        out_ref[g, 0:16] = (point0[16 * g : 16 * g + 16] + tail).astype(BF)
        out_ref[g, 48:64] = last
    grad[...] = dot(near_ref[...], stack[...])
    for rows in chunks():
        tile_grad = jnp.where(live_at(side_ref, rows), masked_ref[rows] + grad[rows], 0.0)
        stack[rows] = tile_grad.astype(BF)
    proj = dot_tn(slots_ref[:, HALF:], stack[0:ALL]).astype(BF)
    for g in range(PLANE):
        out_ref[g, 32:48] = proj[16 * g : 16 * g + 16]


def finish(in_ref, proj_ref, point_ref, depth_ref, bias_ref):
    sums = []
    for r in range(0, 64, 16):
        total = in_ref[0, r : r + 16].astype(F32)
        for g in range(1, PLANE):
            total = total + in_ref[g, r : r + 16].astype(F32)
        sums.append(total)
    proj_ref[...] = sums[2]
    for layer in range(2):
        for i in range(COLS):
            point_ref[i, layer : layer + 1] = sums[layer][i : i + 1]
    for t in range(9):
        depth_ref[t, 0:1] = sums[3][11 + t : 12 + t] if t < 5 else sums[0][7 + t : 8 + t]
        depth_ref[t, 1:2] = sums[3][t : t + 1]
    bias_ref[1:2] = sums[3][9:10]
    bias_ref[0:1] = sums[3][10:11]


def call(body, outs, specs, *args, scratch=(), out_specs=None, mib=20):
    return pl.pallas_call(
        body, out_shape=[jax.ShapeDtypeStruct(s, d) for s, d in outs], in_specs=specs,
        out_specs=out_specs or [VM] * len(outs), scratch_shapes=list(scratch),
        compiler_params=pltpu.CompilerParams(vmem_limit_bytes=mib * 1024 * 1024),
        name=body.__name__)(*args)


def swap(value):
    return lax.ppermute(value, "pipe", [(0, 1), (1, 0)])


def shards(tiles, counts, cells, block_in, block_out, proj, depth, point, bias, cotangent):
    depth = depth.transpose(1, 0, 2)
    x = tiles.reshape(ROWS * POS, CH)
    (x,) = call(
        first_section, [(x.shape, BF)], [HB] * 3, x, block_in, block_out, mib=60,
        scratch=[pltpu.VMEM(x.shape, BF), pltpu.VMEM((CH, 512), BF), pltpu.VMEM((512, CH), BF),
                 pltpu.SemaphoreType.DMA((3, 4))])
    x = lax.ppermute(x, "pipe", [(0, 1)])
    (own_side,) = call(side_rows, [((NZ, ROWS, SIDE), BF)], [SM, SM, VM], cells, counts, cotangent)
    side = lax.all_to_all(own_side, "z", 0, 0, tiled=True).reshape(ALL, SIDE)
    (mine,) = call(second_section, [((ROWS, CH), BF)], [VM, HB, HB], x, block_in, block_out,
                   scratch=[pltpu.VMEM((CH, 512), BF), pltpu.VMEM((512, CH), BF),
                            pltpu.SemaphoreType.DMA((2, 2))], mib=52)
    got = lax.ppermute(mine, "pipe", [(1, 0)])
    (slots,) = call(project, [((NZ, ROWS, WIDTH), BF)], [VM] * 4, own_side, mine, got, proj)
    slots = lax.all_to_all(slots, "z", 0, 0, tiled=True).reshape(ALL, WIDTH)
    half_b, half_f = ((ALL, HALF), BF), ((ALL, HALF), F32)
    hits, long_hits = ((ALL, 9 * ALL), BF), ((9 * ALL, ALL), BF)
    near, near_long, far, far_long = call(
        taps, [hits, long_hits, hits, long_hits], [VM], side)
    stack = pltpu.VMEM((9 * ALL, HALF), BF)
    moved, grad = pltpu.VMEM((9 * ALL, HALF), F32), pltpu.VMEM((ALL, HALF), F32)
    sem = pltpu.SemaphoreType.DMA
    spread0, part, send = call(
        layer0, [half_b, half_f, half_b], [VM] * 3 + [HB], slots, depth, near,
        point, scratch=[stack, pltpu.VMEM((HALF, FEAT), BF), sem], mib=48)
    pre0, grid1, spread1, part, send = call(
        layer1, [half_f, half_b, half_b, half_f, half_b], [VM] * 7 + [HB],
        slots, side, part, swap(send), depth, bias, far, point,
        scratch=[stack, pltpu.VMEM((HALF, FEAT), BF), sem], mib=48)
    mixed, slope1, sum1 = call(
        head, [((MB, 1, CELLS, HALF), BF), half_b, ((1, HALF), F32)], [VM] * 5,
        side, part, swap(send), grid1, bias, out_specs=[HB, VM, VM],
        scratch=[pltpu.VMEM((MB, 1, CELLS, HALF), BF), sem])
    got1 = swap(slope1)
    masked, slope0, grads = call(
        back1, [half_f, half_b, ((16, HALF), F32)], [VM] * 10,
        side, slope1, got1, grid1, pre0, sum1, depth, far, far_long, point,
        scratch=[stack, moved, grad])
    (sums,) = call(
        back0, [((PLANE, 64, HALF), BF)], [VM] * 14,
        slots, side, slope0, swap(slope0), slope1, got1, spread0, spread1, masked, grads, depth,
        near, near_long, point,
        scratch=[stack, moved, grad, pltpu.VMEM((32, HALF), F32)])
    sums = lax.all_to_all(sums, ("y", "x"), 0, 0, tiled=True)
    grad_proj, grad_point, grad_depth, grad_bias = call(
        finish, [((16, HALF), F32), ((COLS, 2, HALF), F32), ((9, 2, HALF), F32), ((2, HALF), F32)],
        [VM], sums)
    return (mixed, grad_proj, grad_point.transpose(1, 2, 0), grad_depth.transpose(1, 0, 2), grad_bias)


def solution(mesh):
    grid = Mesh(mesh.devices.reshape(2, NZ, NY, NX), ("pipe", "z", "y", "x"))
    dp = ("z", "y", "x")
    in_specs = (
        P(None, dp, None, None, None),
        P(None, dp),
        P(None, dp, None),
        P("pipe", None, None),
        P("pipe", None, None),
        P(None, "pipe"),
        P(None, None, "pipe"),
        P(None, "pipe", None),
        P(None, "pipe"),
        P(None, dp, None, "pipe"),
    )
    out_specs = (
        P(None, dp, None, "pipe"),
        P(dp, "pipe"),
        P(None, "pipe", dp),
        P(None, None, "pipe"),
        P(None, "pipe"),
    )
    return jax.shard_map(shards, mesh=grid, in_specs=in_specs, out_specs=out_specs, check_vma=False)
```

```python
import jax
import jax.numpy as jnp
from jax import lax
from jax.experimental import pallas as pl
from jax.experimental.pallas import tpu as pltpu
from jax.sharding import Mesh, PartitionSpec as P

MB = 2
OWN = 16
POS = 8
ROWS = MB * OWN
CH = 2048
FEAT = 1536
HALF = 768
CELLS = 256
NZ, NY, NX = 8, 4, 4
PLANE = NY * NX
ALL = NZ * ROWS
SLICE = CH // NZ
COLS = 12
WIDTH = HALF + SLICE
SIDE = HALF + 128
STEP = 16
BF = jnp.bfloat16
F32 = jnp.float32
VM = pl.BlockSpec(memory_space=pltpu.VMEM)
HB = pl.BlockSpec(memory_space=pltpu.HBM)
SM = pl.BlockSpec(memory_space=pltpu.SMEM)


def dot(a, b):
    return jnp.dot(a, b, preferred_element_type=F32)


def dot_nt(a, b):
    return lax.dot_general(a, b, (((1,), (1,)), ((), ())), preferred_element_type=F32)


def dot_tn(a, b):
    return lax.dot_general(a, b, (((0,), (0,)), ((), ())), preferred_element_type=F32)


def iota(shape, axis):
    return lax.broadcasted_iota(jnp.int32, shape, axis)


def halves():
    p = lax.axis_index("pipe")
    mine = pl.multiple_of(p * HALF, 128)
    other = pl.multiple_of((1 - p) * HALF, 128)
    return pl.ds(mine, HALF), pl.ds(other, HALF)


def own_live(counts_ref, width):
    rows = iota((ROWS, width), 0)
    return (rows & (OWN - 1)) < jnp.where(rows < OWN, counts_ref[0, 0], counts_ref[1, 0])


def wide(code, times):
    return jnp.concatenate([code.astype(F32)] * times, axis=1)


def live_at(side_ref, rows):
    return wide(side_ref[rows, HALF:], HALF // 128) >= 0


def taps(side_ref, near_ref, near_long_ref, far_ref, far_long_ref):
    code = wide(side_ref[:, HALF:], 2)
    rows, cols = code.astype(jnp.int32), code.T.astype(jnp.int32)
    block = (iota((ALL, ALL), 0) >> 4) == (iota((ALL, ALL), 1) >> 4)
    pair = block & (rows >= 0) & (cols >= 0)
    down = jnp.where(pair, (cols >> 4) - (rows >> 4), 64)
    right = (cols & 15) - (rows & 15)
    for dilation, out_ref, long_ref in ((2, near_ref, near_long_ref), (4, far_ref, far_long_ref)):
        for t in range(9):
            hit = (down == (t // 3 - 1) * dilation) & (right == (t % 3 - 1) * dilation)
            hit = jnp.where(hit, 1.0, 0.0).astype(BF)
            out_ref[:, t * ALL : (t + 1) * ALL] = hit
            long_ref[t * ALL : (t + 1) * ALL] = hit


def chunks():
    return [slice(i, i + STEP) for i in range(0, ALL, STEP)]


def put_weighed(stack, rows, value, depth_ref, layer, backward):
    for t in range(9):
        s = 8 - t if backward else t
        at = slice(t * ALL + rows.start, t * ALL + rows.stop)
        stack[at] = (value * depth_ref[s, layer : layer + 1, :]).astype(BF)


def depth_rows(grad, moved, out_ref, rows):
    for at in (slice(0, 384), slice(384, HALF)):
        sums = [None] * 9
        for i in range(0, ALL, 8):
            value = grad[i : i + 8, at]
            for t in range(9):
                term = moved[t * ALL + i : t * ALL + i + 8, at] * value
                sums[t] = term if sums[t] is None else sums[t] + term
        for t in range(9):
            out_ref[rows[t] : rows[t] + 1, at] = jnp.sum(sums[t], axis=0, keepdims=True)


def gelu_parts(x):
    c = 0.7978845608028654
    t = jnp.tanh(c * (x + 0.044715 * (x * x * x)))
    half = 0.5 * (1.0 + t)
    slope = half + 0.5 * x * (1.0 - t * t) * (c * (1.0 + 3 * 0.044715 * (x * x)))
    return x * half, slope


def encode(x_ref, w_in_ref, w_out_ref):
    x = x_ref[...]
    hidden = jnp.maximum(dot(x, w_in_ref[0]), 0.0).astype(BF)
    return jnp.maximum(x.astype(F32) + dot(hidden, w_out_ref[0]), 0.0).astype(BF)


def side_rows(cells_ref, counts_ref, cot_ref, out_ref, code_ref):
    rows = iota((ROWS, 128), 0)
    code = jnp.zeros((ROWS, 128), jnp.int32)
    for m in range(MB):
        for j in range(OWN):
            code = jnp.where(rows == m * OWN + j, cells_ref[m, 0, j], code)
    code = jnp.where(own_live(counts_ref, 128), code, -1)
    double = jnp.concatenate([code, code], axis=1)
    code = code.astype(F32).astype(BF)
    code_ref[...] = code
    hit = jnp.where(double == iota((ROWS, CELLS), 1), 1.0, 0.0).astype(BF)
    for m in range(MB):
        at = slice(m * OWN, (m + 1) * OWN)
        cot = dot(hit[at], cot_ref[m, 0]).astype(BF)
        for z in range(NZ):
            out_ref[z, at, :HALF] = cot
            out_ref[z, at, HALF:] = code[at]


def first_section(cells_ref, counts_ref, cot_hbm, x_hbm, w_in_hbm, w_out_hbm, out_ref, side_hbm,
                  code_ref, cot_ref, side_ref, x_ref, w_in_ref, w_out_ref, sems):
    n = 4
    step = CH // n
    first = pltpu.make_async_copy(cot_hbm, cot_ref, sems.at[3, 0])
    last = pltpu.make_async_copy(side_ref, side_hbm, sems.at[3, 1])
    copies = []
    for k in range(n):
        at = pl.ds(k * step, step)
        copies.append(pltpu.make_async_copy(x_hbm.at[:, at], x_ref.at[:, at], sems.at[0, k]))
        copies.append(pltpu.make_async_copy(w_in_hbm.at[0, at], w_in_ref.at[at], sems.at[1, k]))
    for k in range(n):
        at = pl.ds(k * step, step)
        copies.append(
            pltpu.make_async_copy(w_out_hbm.at[0, :, at], w_out_ref.at[:, at], sems.at[2, k]))
    for copy in [first] + copies:
        copy.start()
    first.wait()
    side_rows(cells_ref, counts_ref, cot_ref, side_ref, code_ref)
    last.start()
    hidden = None
    for k in range(n):
        at = slice(k * step, (k + 1) * step)
        copies[2 * k].wait()
        copies[2 * k + 1].wait()
        part = dot(x_ref[:, at], w_in_ref[at])
        hidden = part if hidden is None else hidden + part
    hidden = jnp.maximum(hidden, 0.0).astype(BF)
    for k in range(n):
        at = slice(k * step, (k + 1) * step)
        copies[2 * n + k].wait()
        total = x_ref[:, at].astype(F32) + dot(hidden, w_out_ref[:, at])
        out_ref[:, at] = jnp.maximum(total, 0.0).astype(BF)
    last.wait()


def second_section(x_ref, w_in_hbm, w_out_hbm, out_ref, w_in_ref, w_out_ref, sems):
    n = ROWS * POS
    ins, outs = [], []
    for k in range(2):
        at = pl.ds(k * (CH // 2), CH // 2)
        ins.append(pltpu.make_async_copy(w_in_hbm.at[0, at], w_in_ref.at[at], sems.at[0, k]))
        outs.append(
            pltpu.make_async_copy(w_out_hbm.at[0, :, at], w_out_ref.at[:, at], sems.at[1, k]))
    for copy in ins + outs:
        copy.start()
    pool = jnp.where(iota((ROWS, n), 1) >> 3 == iota((ROWS, n), 0), 1.0 / POS, 0.0).astype(BF)
    hidden = None
    for k in range(2):
        at = slice(k * (CH // 2), (k + 1) * (CH // 2))
        ins[k].wait()
        part = dot(x_ref[:, at], w_in_ref[at])
        hidden = part if hidden is None else hidden + part
    hidden = jnp.maximum(hidden, 0.0).astype(BF)
    for k in range(2):
        at = slice(k * (CH // 2), (k + 1) * (CH // 2))
        outs[k].wait()
        total = x_ref[:, at].astype(F32) + dot(hidden, w_out_ref[:, at])
        out_ref[:, at] = dot(pool, jnp.maximum(total, 0.0).astype(BF)).astype(BF)


def project(code_ref, mine_ref, got_ref, proj_ref, out_hbm, out_ref, sems):
    pooled = jnp.where(lax.axis_index("pipe") == 1, mine_ref[...], got_ref[...])
    for z in range(NZ):
        out_ref[z, :, HALF:] = pooled[:, z * SLICE : (z + 1) * SLICE]
    copies = []
    for i, at in enumerate((pl.ds(HALF, SLICE), pl.ds(0, HALF))):
        copies.append(
            pltpu.make_async_copy(out_ref.at[:, :, at], out_hbm.at[:, :, at], sems.at[i]))
    copies[0].start()
    live = wide(code_ref[...], HALF // 128) >= 0
    feat = jnp.where(live, dot(pooled, proj_ref[...]), 0.0).astype(BF)
    for z in range(NZ):
        out_ref[z, :, :HALF] = feat
    copies[1].start()
    for copy in copies:
        copy.wait()


def mix(spread_ref, w, part_ref, send_ref):
    mine, other = halves()
    send_ref[...] = dot(spread_ref[...], w[:, other]).astype(BF)
    part_ref[...] = dot(spread_ref[...], w[:, mine])


def unmix(slope_ref, got_ref, w):
    mine, other = halves()
    return dot_nt(slope_ref[...], w[:, mine]) + dot_nt(got_ref[...], w[:, other])


def layer0(slots_ref, depth_ref, near_ref, point_ref, spread_ref, part_ref, send_ref, next_ref,
           stack, w, sems):
    copy = pltpu.make_async_copy(point_ref.at[0], w, sems.at[0])
    copy.start()
    later = pltpu.make_async_copy(point_ref.at[1], next_ref, sems.at[1])
    later.start()
    for rows in chunks():
        put_weighed(stack, rows, slots_ref[rows, :HALF].astype(F32), depth_ref, 0, False)
    spread_ref[...] = dot(near_ref[...], stack[...]).astype(BF)
    copy.wait()
    mix(spread_ref, w, part_ref, send_ref)
    later.wait()


def layer1(slots_ref, side_ref, part_ref, got_ref, depth_ref, bias_ref, far_ref, point_ref,
           pre_ref, grid_ref, spread_ref, part_out_ref, send_ref, stack):
    for rows in chunks():
        pre = part_ref[rows] + got_ref[rows].astype(F32) + bias_ref[0:1]
        pre_ref[rows] = pre
        value = slots_ref[rows, :HALF].astype(F32) + gelu_parts(pre)[0]
        grid = jnp.where(live_at(side_ref, rows), value, 0.0).astype(BF)
        grid_ref[rows] = grid
        put_weighed(stack, rows, grid.astype(F32), depth_ref, 1, False)
    spread_ref[...] = dot(far_ref[...], stack[...]).astype(BF)
    mix(spread_ref, point_ref, part_out_ref, send_ref)


def head(side_ref, part_ref, got_ref, grid_ref, bias_ref,
         mixed_ref, slope_ref, sum_ref, mixed, sem):
    for m in range(MB):
        at = pl.ds(pl.multiple_of(lax.axis_index("z") * ROWS + m * OWN, OWN), OWN)
        pre = part_ref[at] + got_ref[at].astype(F32) + bias_ref[1:2]
        rows = (grid_ref[at].astype(F32) + gelu_parts(pre)[0]).astype(BF)
        code = wide(side_ref[at, HALF:], 2).astype(jnp.int32)
        hit = jnp.where(code == iota((OWN, CELLS), 1), 1.0, 0.0).astype(BF)
        mixed[m, 0] = dot_tn(hit, rows).astype(BF)
    out = pltpu.make_async_copy(mixed, mixed_ref, sem)
    out.start()
    total = None
    for rows in chunks():
        pre = part_ref[rows] + got_ref[rows].astype(F32) + bias_ref[1:2]
        slope = side_ref[rows, :HALF].astype(F32) * gelu_parts(pre)[1]
        slope = jnp.where(live_at(side_ref, rows), slope, 0.0)
        slope_ref[rows] = slope.astype(BF)
        total = slope if total is None else total + slope
    sum_ref[...] = jnp.sum(total, axis=0, keepdims=True)
    out.wait()


def back1(side_ref, slope_ref, got_ref, grid_ref, pre_ref, sum_ref, depth_ref, far_ref,
          far_long_ref, point_ref, masked_ref, out_ref, grads_ref, stack, moved, grad):
    grad[...] = unmix(slope_ref, got_ref, point_ref)
    for rows in chunks():
        put_weighed(stack, rows, grad[rows], depth_ref, 1, True)
    grads_ref[...] = jnp.zeros((16, HALF), F32)
    moved[...] = dot(far_long_ref[...], grid_ref[...])
    depth_rows(grad, moved, grads_ref, list(range(9)))
    grad[...] = dot(far_ref[...], stack[...])
    total = None
    for rows in chunks():
        masked = side_ref[rows, :HALF].astype(F32) + grad[rows]
        masked = jnp.where(live_at(side_ref, rows), masked, 0.0)
        masked_ref[rows] = masked
        slope = masked * gelu_parts(pre_ref[rows])[1]
        out_ref[rows] = slope.astype(BF)
        total = slope if total is None else total + slope
    grads_ref[9:10] = sum_ref[...]
    grads_ref[10:11] = jnp.sum(total, axis=0, keepdims=True)


def slope_rows(side, values):
    row = iota((256, 1), 0)
    group, i = row >> 4, row & 15
    column = lax.axis_index("z") * 192 + group * COLS + i - side * HALF
    column = jnp.where(i < COLS, column, -1)
    picker = jnp.where(iota((256, HALF), 1) == column, 1.0, 0.0).astype(BF)
    return [dot_nt(picker, value) for value in values]


def back0(slots_ref, side_ref, slope_ref, got_ref, slope1_ref, got1_ref, spread0_ref, spread1_ref,
          masked_ref, grads_ref, depth_ref, near_ref, near_long_ref, point_ref, out_ref,
          stack, moved, grad, grads, w, sem):
    copy = pltpu.make_async_copy(point_ref.at[0], w, sem)
    copy.start()
    p = lax.axis_index("pipe")
    own = slope_rows(p, (slope_ref[...], slope1_ref[...]))
    far = slope_rows(1 - p, (got_ref[...], got1_ref[...]))
    point0 = dot((own[0] + far[0]).astype(BF), spread0_ref[...])
    point1 = dot((own[1] + far[1]).astype(BF), spread1_ref[...]).astype(BF)
    for g in range(PLANE):
        out_ref[g, 16:32] = point1[16 * g : 16 * g + 16]
    moved[...] = dot(near_long_ref[...], slots_ref[:, :HALF])
    copy.wait()
    grad[...] = unmix(slope_ref, got_ref, w)
    for rows in chunks():
        put_weighed(stack, rows, grad[rows], depth_ref, 0, True)
    grads[0:16] = grads_ref[...]
    grads[16:32] = jnp.zeros((16, HALF), F32)
    where = [11 + t if t < 5 else 23 + t for t in range(9)]
    depth_rows(grad, moved, grads, where)
    tail, last = grads[16:32], grads[0:16].astype(BF)
    for g in range(PLANE):
        out_ref[g, 0:16] = (point0[16 * g : 16 * g + 16] + tail).astype(BF)
        out_ref[g, 48:64] = last
    grad[...] = dot(near_ref[...], stack[...])
    for rows in chunks():
        tile_grad = jnp.where(live_at(side_ref, rows), masked_ref[rows] + grad[rows], 0.0)
        stack[rows] = tile_grad.astype(BF)
    proj = dot_tn(slots_ref[:, HALF:], stack[0:ALL]).astype(BF)
    for g in range(PLANE):
        out_ref[g, 32:48] = proj[16 * g : 16 * g + 16]


def finish(in_ref, proj_ref, point_ref, depth_ref, bias_ref):
    sums = []
    for r in range(0, 64, 16):
        total = in_ref[0, r : r + 16].astype(F32)
        for g in range(1, PLANE):
            total = total + in_ref[g, r : r + 16].astype(F32)
        sums.append(total)
    proj_ref[...] = sums[2]
    for layer in range(2):
        for i in range(COLS):
            point_ref[i, layer : layer + 1] = sums[layer][i : i + 1]
    for t in range(9):
        depth_ref[t, 0:1] = sums[3][11 + t : 12 + t] if t < 5 else sums[0][7 + t : 8 + t]
        depth_ref[t, 1:2] = sums[3][t : t + 1]
    bias_ref[1:2] = sums[3][9:10]
    bias_ref[0:1] = sums[3][10:11]


def call(body, outs, specs, *args, scratch=(), out_specs=None, mib=20):
    return pl.pallas_call(
        body, out_shape=[jax.ShapeDtypeStruct(s, d) for s, d in outs], in_specs=specs,
        out_specs=out_specs or [VM] * len(outs), scratch_shapes=list(scratch),
        compiler_params=pltpu.CompilerParams(vmem_limit_bytes=mib * 1024 * 1024),
        name=body.__name__)(*args)


def swap(value):
    return lax.ppermute(value, "pipe", [(0, 1), (1, 0)])


def shards(tiles, counts, cells, block_in, block_out, proj, depth, point, bias, cotangent):
    depth = depth.transpose(1, 0, 2)
    x = tiles.reshape(ROWS * POS, CH)
    x, own_side, code = call(
        first_section, [(x.shape, BF), ((NZ, ROWS, SIDE), BF), ((ROWS, 128), BF)],
        [SM, SM] + [HB] * 4, cells, counts, cotangent, x, block_in, block_out, mib=60,
        out_specs=[VM, HB, VM],
        scratch=[pltpu.VMEM(cotangent.shape, BF), pltpu.VMEM((NZ, ROWS, SIDE), BF),
                 pltpu.VMEM(x.shape, BF), pltpu.VMEM((CH, 512), BF), pltpu.VMEM((512, CH), BF),
                 pltpu.SemaphoreType.DMA((4, 4))])
    x = lax.ppermute(x, "pipe", [(0, 1)])
    side = lax.all_to_all(own_side, "z", 0, 0, tiled=True).reshape(ALL, SIDE)
    (mine,) = call(second_section, [((ROWS, CH), BF)], [VM, HB, HB], x, block_in, block_out,
                   scratch=[pltpu.VMEM((CH, 512), BF), pltpu.VMEM((512, CH), BF),
                            pltpu.SemaphoreType.DMA((2, 2))], mib=52)
    got = lax.ppermute(mine, "pipe", [(1, 0)])
    (slots,) = call(
        project, [((NZ, ROWS, WIDTH), BF)], [VM] * 4, code, mine, got, proj, out_specs=[HB],
        scratch=[pltpu.VMEM((NZ, ROWS, WIDTH), BF), pltpu.SemaphoreType.DMA((2,))])
    slots = lax.all_to_all(slots, "z", 0, 0, tiled=True).reshape(ALL, WIDTH)
    half_b, half_f = ((ALL, HALF), BF), ((ALL, HALF), F32)
    hits, long_hits = ((ALL, 9 * ALL), BF), ((9 * ALL, ALL), BF)
    near, near_long, far, far_long = call(
        taps, [hits, long_hits, hits, long_hits], [VM], side)
    stack = pltpu.VMEM((9 * ALL, HALF), BF)
    moved, grad = pltpu.VMEM((9 * ALL, HALF), F32), pltpu.VMEM((ALL, HALF), F32)
    sem = pltpu.SemaphoreType.DMA
    spread0, part, send, point1 = call(
        layer0, [half_b, half_f, half_b, ((HALF, FEAT), BF)], [VM] * 3 + [HB], slots, depth, near,
        point, scratch=[stack, pltpu.VMEM((HALF, FEAT), BF), pltpu.SemaphoreType.DMA((2,))],
        mib=48)
    pre0, grid1, spread1, part, send = call(
        layer1, [half_f, half_b, half_b, half_f, half_b], [VM] * 8,
        slots, side, part, swap(send), depth, bias, far, point1, scratch=[stack])
    mixed, slope1, sum1 = call(
        head, [((MB, 1, CELLS, HALF), BF), half_b, ((1, HALF), F32)], [VM] * 5,
        side, part, swap(send), grid1, bias, out_specs=[HB, VM, VM],
        scratch=[pltpu.VMEM((MB, 1, CELLS, HALF), BF), sem])
    got1 = swap(slope1)
    masked, slope0, grads = call(
        back1, [half_f, half_b, ((16, HALF), F32)], [VM] * 10,
        side, slope1, got1, grid1, pre0, sum1, depth, far, far_long, point1,
        scratch=[stack, moved, grad])
    (sums,) = call(
        back0, [((PLANE, 64, HALF), BF)], [VM] * 13 + [HB],
        slots, side, slope0, swap(slope0), slope1, got1, spread0, spread1, masked, grads, depth,
        near, near_long, point,
        scratch=[stack, moved, grad, pltpu.VMEM((32, HALF), F32), pltpu.VMEM((HALF, FEAT), BF), sem],
        mib=44)
    sums = lax.all_to_all(sums, ("y", "x"), 0, 0, tiled=True)
    grad_proj, grad_point, grad_depth, grad_bias = call(
        finish, [((16, HALF), F32), ((COLS, 2, HALF), F32), ((9, 2, HALF), F32), ((2, HALF), F32)],
        [VM], sums)
    return (mixed, grad_proj, grad_point.transpose(1, 2, 0), grad_depth.transpose(1, 0, 2), grad_bias)


def solution(mesh):
    grid = Mesh(mesh.devices.reshape(2, NZ, NY, NX), ("pipe", "z", "y", "x"))
    dp = ("z", "y", "x")
    in_specs = (
        P(None, dp, None, None, None),
        P(None, dp),
        P(None, dp, None),
        P("pipe", None, None),
        P("pipe", None, None),
        P(None, "pipe"),
        P(None, None, "pipe"),
        P(None, "pipe", None),
        P(None, "pipe"),
        P(None, dp, None, "pipe"),
    )
    out_specs = (
        P(None, dp, None, "pipe"),
        P(dp, "pipe"),
        P(None, "pipe", dp),
        P(None, None, "pipe"),
        P(None, "pipe"),
    )
    return jax.shard_map(shards, mesh=grid, in_specs=in_specs, out_specs=out_specs, check_vma=False)
```

```python
import jax
import jax.numpy as jnp
from jax import lax
from jax.experimental import pallas as pl
from jax.experimental.pallas import tpu as pltpu
from jax.sharding import Mesh, PartitionSpec as P

MB = 2
OWN = 16
POS = 8
ROWS = MB * OWN
CH = 2048
FEAT = 1536
HALF = 768
CELLS = 256
NZ, NY, NX = 8, 4, 4
PLANE = NY * NX
ALL = NZ * ROWS
SLICE = CH // NZ
COLS = 12
WIDTH = HALF + SLICE
SIDE = HALF + 128
STEP = 16
BF = jnp.bfloat16
F32 = jnp.float32
VM = pl.BlockSpec(memory_space=pltpu.VMEM)
HB = pl.BlockSpec(memory_space=pltpu.HBM)
SM = pl.BlockSpec(memory_space=pltpu.SMEM)


def dot(a, b):
    return jnp.dot(a, b, preferred_element_type=F32)


def dot_nt(a, b):
    return lax.dot_general(a, b, (((1,), (1,)), ((), ())), preferred_element_type=F32)


def dot_tn(a, b):
    return lax.dot_general(a, b, (((0,), (0,)), ((), ())), preferred_element_type=F32)


def iota(shape, axis):
    return lax.broadcasted_iota(jnp.int32, shape, axis)


def halves():
    p = lax.axis_index("pipe")
    mine = pl.multiple_of(p * HALF, 128)
    other = pl.multiple_of((1 - p) * HALF, 128)
    return pl.ds(mine, HALF), pl.ds(other, HALF)


def own_live(counts_ref, width):
    rows = iota((ROWS, width), 0)
    return (rows & (OWN - 1)) < jnp.where(rows < OWN, counts_ref[0, 0], counts_ref[0, 1])


def wide(code, times):
    return jnp.concatenate([code.astype(F32)] * times, axis=1)


def live_at(side_ref, rows):
    return wide(side_ref[rows, HALF:], HALF // 128) >= 0


def taps(side_ref, near_ref, near_long_ref, far_ref, far_long_ref):
    code = wide(side_ref[:, HALF:], 2)
    rows, cols = code.astype(jnp.int32), code.T.astype(jnp.int32)
    block = (iota((ALL, ALL), 0) >> 4) == (iota((ALL, ALL), 1) >> 4)
    pair = block & (rows >= 0) & (cols >= 0)
    down = jnp.where(pair, (cols >> 4) - (rows >> 4), 64)
    right = (cols & 15) - (rows & 15)
    for dilation, out_ref, long_ref in ((2, near_ref, near_long_ref), (4, far_ref, far_long_ref)):
        for t in range(9):
            hit = (down == (t // 3 - 1) * dilation) & (right == (t % 3 - 1) * dilation)
            hit = jnp.where(hit, 1.0, 0.0).astype(BF)
            out_ref[:, t * ALL : (t + 1) * ALL] = hit
            long_ref[t * ALL : (t + 1) * ALL] = hit


def chunks():
    return [slice(i, i + STEP) for i in range(0, ALL, STEP)]


def put_weighed(stack, rows, value, depth_ref, layer, backward):
    for t in range(9):
        s = 8 - t if backward else t
        at = slice(t * ALL + rows.start, t * ALL + rows.stop)
        stack[at] = (value * depth_ref[s, layer : layer + 1, :]).astype(BF)


def depth_rows(grad, moved, out_ref, rows):
    for at in (slice(0, 384), slice(384, HALF)):
        sums = [None] * 9
        for i in range(0, ALL, 8):
            value = grad[i : i + 8, at]
            for t in range(9):
                term = moved[t * ALL + i : t * ALL + i + 8, at] * value
                sums[t] = term if sums[t] is None else sums[t] + term
        for t in range(9):
            out_ref[rows[t] : rows[t] + 1, at] = jnp.sum(sums[t], axis=0, keepdims=True)


def gelu_parts(x):
    c = 0.7978845608028654
    t = jnp.tanh(c * (x + 0.044715 * (x * x * x)))
    half = 0.5 * (1.0 + t)
    slope = half + 0.5 * x * (1.0 - t * t) * (c * (1.0 + 3 * 0.044715 * (x * x)))
    return x * half, slope


def encode(x_ref, w_in_ref, w_out_ref):
    x = x_ref[...]
    hidden = jnp.maximum(dot(x, w_in_ref[0]), 0.0).astype(BF)
    return jnp.maximum(x.astype(F32) + dot(hidden, w_out_ref[0]), 0.0).astype(BF)


def side_rows(cells_ref, counts_ref, cot_ref, out_ref, code_ref):
    rows = iota((ROWS, 128), 0)
    code = jnp.zeros((ROWS, 128), jnp.int32)
    for m in range(MB):
        for j in range(OWN):
            code = jnp.where(rows == m * OWN + j, cells_ref[m, 0, j], code)
    code = jnp.where(own_live(counts_ref, 128), code, -1)
    double = jnp.concatenate([code, code], axis=1)
    code = code.astype(F32).astype(BF)
    code_ref[...] = code
    hit = jnp.where(double == iota((ROWS, CELLS), 1), 1.0, 0.0).astype(BF)
    for m in range(MB):
        at = slice(m * OWN, (m + 1) * OWN)
        cot = dot(hit[at], cot_ref[m, 0]).astype(BF)
        for z in range(NZ):
            out_ref[z, at, :HALF] = cot
            out_ref[z, at, HALF:] = code[at]


def first_section(cells_ref, counts_ref, cot_hbm, x_hbm, w_in_hbm, w_out_hbm, out_ref, side_hbm,
                  code_ref, cot_ref, side_ref, x_ref, w_in_ref, w_out_ref, sems):
    n = 4
    step = CH // n
    first = pltpu.make_async_copy(cot_hbm, cot_ref, sems.at[3, 0])
    last = pltpu.make_async_copy(side_ref, side_hbm, sems.at[3, 1])
    copies = []
    for k in range(n):
        at = pl.ds(k * step, step)
        copies.append(pltpu.make_async_copy(x_hbm.at[:, at], x_ref.at[:, at], sems.at[0, k]))
        copies.append(pltpu.make_async_copy(w_in_hbm.at[0, at], w_in_ref.at[at], sems.at[1, k]))
    for k in range(n):
        at = pl.ds(k * step, step)
        copies.append(
            pltpu.make_async_copy(w_out_hbm.at[0, :, at], w_out_ref.at[:, at], sems.at[2, k]))
    for copy in [first] + copies:
        copy.start()
    first.wait()
    side_rows(cells_ref, counts_ref, cot_ref, side_ref, code_ref)
    last.start()
    hidden = None
    for k in range(n):
        at = slice(k * step, (k + 1) * step)
        copies[2 * k].wait()
        copies[2 * k + 1].wait()
        part = dot(x_ref[:, at], w_in_ref[at])
        hidden = part if hidden is None else hidden + part
    hidden = jnp.maximum(hidden, 0.0).astype(BF)
    for k in range(n):
        at = slice(k * step, (k + 1) * step)
        copies[2 * n + k].wait()
        total = x_ref[:, at].astype(F32) + dot(hidden, w_out_ref[:, at])
        out_ref[:, at] = jnp.maximum(total, 0.0).astype(BF)
    last.wait()


def second_section(x_ref, w_in_hbm, w_out_hbm, out_ref, w_in_ref, w_out_ref, sems):
    n = ROWS * POS
    ins, outs = [], []
    for k in range(2):
        at = pl.ds(k * (CH // 2), CH // 2)
        ins.append(pltpu.make_async_copy(w_in_hbm.at[0, at], w_in_ref.at[at], sems.at[0, k]))
        outs.append(
            pltpu.make_async_copy(w_out_hbm.at[0, :, at], w_out_ref.at[:, at], sems.at[1, k]))
    for copy in ins + outs:
        copy.start()
    pool = jnp.where(iota((ROWS, n), 1) >> 3 == iota((ROWS, n), 0), 1.0 / POS, 0.0).astype(BF)
    hidden = None
    for k in range(2):
        at = slice(k * (CH // 2), (k + 1) * (CH // 2))
        ins[k].wait()
        part = dot(x_ref[:, at], w_in_ref[at])
        hidden = part if hidden is None else hidden + part
    hidden = jnp.maximum(hidden, 0.0).astype(BF)
    for k in range(2):
        at = slice(k * (CH // 2), (k + 1) * (CH // 2))
        outs[k].wait()
        total = x_ref[:, at].astype(F32) + dot(hidden, w_out_ref[:, at])
        out_ref[:, at] = dot(pool, jnp.maximum(total, 0.0).astype(BF)).astype(BF)


def project(code_ref, mine_ref, got_ref, proj_ref, out_hbm, out_ref, sems):
    pooled = jnp.where(lax.axis_index("pipe") == 1, mine_ref[...], got_ref[...])
    for z in range(NZ):
        out_ref[z, :, HALF:] = pooled[:, z * SLICE : (z + 1) * SLICE]
    copies = []
    for i, at in enumerate((pl.ds(HALF, SLICE), pl.ds(0, HALF))):
        copies.append(
            pltpu.make_async_copy(out_ref.at[:, :, at], out_hbm.at[:, :, at], sems.at[i]))
    copies[0].start()
    live = wide(code_ref[...], HALF // 128) >= 0
    feat = jnp.where(live, dot(pooled, proj_ref[...]), 0.0).astype(BF)
    for z in range(NZ):
        out_ref[z, :, :HALF] = feat
    copies[1].start()
    for copy in copies:
        copy.wait()


def mix(spread_ref, w, part_ref, send_ref):
    mine, other = halves()
    send_ref[...] = dot(spread_ref[...], w[:, other]).astype(BF)
    part_ref[...] = dot(spread_ref[...], w[:, mine])


def unmix(slope_ref, got_ref, w):
    mine, other = halves()
    return dot_nt(slope_ref[...], w[:, mine]) + dot_nt(got_ref[...], w[:, other])


def layer0(slots_ref, depth_ref, near_ref, point_ref, spread_ref, part_ref, send_ref, next_ref,
           stack, w, sems):
    copy = pltpu.make_async_copy(point_ref.at[0], w, sems.at[0])
    copy.start()
    later = pltpu.make_async_copy(point_ref.at[1], next_ref, sems.at[1])
    later.start()
    for rows in chunks():
        put_weighed(stack, rows, slots_ref[rows, :HALF].astype(F32), depth_ref, 0, False)
    spread_ref[...] = dot(near_ref[...], stack[...]).astype(BF)
    copy.wait()
    mix(spread_ref, w, part_ref, send_ref)
    later.wait()


def layer1(slots_ref, side_ref, part_ref, got_ref, depth_ref, bias_ref, far_ref, point_ref,
           pre_ref, grid_ref, spread_ref, part_out_ref, send_ref, stack):
    for rows in chunks():
        pre = part_ref[rows] + got_ref[rows].astype(F32) + bias_ref[0:1]
        pre_ref[rows] = pre
        value = slots_ref[rows, :HALF].astype(F32) + gelu_parts(pre)[0]
        grid = jnp.where(live_at(side_ref, rows), value, 0.0).astype(BF)
        grid_ref[rows] = grid
        put_weighed(stack, rows, grid.astype(F32), depth_ref, 1, False)
    spread_ref[...] = dot(far_ref[...], stack[...]).astype(BF)
    mix(spread_ref, point_ref, part_out_ref, send_ref)


def head(side_ref, part_ref, got_ref, grid_ref, bias_ref,
         mixed_ref, slope_ref, sum_ref, mixed, sem):
    for m in range(MB):
        at = pl.ds(pl.multiple_of(lax.axis_index("z") * ROWS + m * OWN, OWN), OWN)
        pre = part_ref[at] + got_ref[at].astype(F32) + bias_ref[1:2]
        rows = (grid_ref[at].astype(F32) + gelu_parts(pre)[0]).astype(BF)
        code = wide(side_ref[at, HALF:], 2).astype(jnp.int32)
        hit = jnp.where(code == iota((OWN, CELLS), 1), 1.0, 0.0).astype(BF)
        mixed[m, 0] = dot_tn(hit, rows).astype(BF)
    out = pltpu.make_async_copy(mixed, mixed_ref, sem)
    out.start()
    total = None
    for rows in chunks():
        pre = part_ref[rows] + got_ref[rows].astype(F32) + bias_ref[1:2]
        slope = side_ref[rows, :HALF].astype(F32) * gelu_parts(pre)[1]
        slope = jnp.where(live_at(side_ref, rows), slope, 0.0)
        slope_ref[rows] = slope.astype(BF)
        total = slope if total is None else total + slope
    sum_ref[...] = jnp.sum(total, axis=0, keepdims=True)
    out.wait()


def back1(side_ref, slope_ref, got_ref, grid_ref, pre_ref, sum_ref, depth_ref, far_ref,
          far_long_ref, point_ref, masked_ref, out_ref, grads_ref, stack, moved, grad):
    grad[...] = unmix(slope_ref, got_ref, point_ref)
    for rows in chunks():
        put_weighed(stack, rows, grad[rows], depth_ref, 1, True)
    grads_ref[...] = jnp.zeros((16, HALF), F32)
    moved[...] = dot(far_long_ref[...], grid_ref[...])
    depth_rows(grad, moved, grads_ref, list(range(9)))
    grad[...] = dot(far_ref[...], stack[...])
    total = None
    for rows in chunks():
        masked = side_ref[rows, :HALF].astype(F32) + grad[rows]
        masked = jnp.where(live_at(side_ref, rows), masked, 0.0)
        masked_ref[rows] = masked
        slope = masked * gelu_parts(pre_ref[rows])[1]
        out_ref[rows] = slope.astype(BF)
        total = slope if total is None else total + slope
    grads_ref[9:10] = sum_ref[...]
    grads_ref[10:11] = jnp.sum(total, axis=0, keepdims=True)


def slope_rows(side, values):
    row = iota((256, 1), 0)
    group, i = row >> 4, row & 15
    column = lax.axis_index("z") * 192 + group * COLS + i - side * HALF
    column = jnp.where(i < COLS, column, -1)
    picker = jnp.where(iota((256, HALF), 1) == column, 1.0, 0.0).astype(BF)
    return [dot_nt(picker, value) for value in values]


def back0(slots_ref, side_ref, slope_ref, got_ref, slope1_ref, got1_ref, spread0_ref, spread1_ref,
          masked_ref, grads_ref, depth_ref, near_ref, near_long_ref, point_ref, out_ref,
          stack, moved, grad, grads, w, sem):
    copy = pltpu.make_async_copy(point_ref.at[0], w, sem)
    copy.start()
    p = lax.axis_index("pipe")
    own = slope_rows(p, (slope_ref[...], slope1_ref[...]))
    far = slope_rows(1 - p, (got_ref[...], got1_ref[...]))
    point0 = dot((own[0] + far[0]).astype(BF), spread0_ref[...])
    point1 = dot((own[1] + far[1]).astype(BF), spread1_ref[...]).astype(BF)
    for g in range(PLANE):
        out_ref[g, 16:32] = point1[16 * g : 16 * g + 16]
    copy.wait()
    grad[...] = unmix(slope_ref, got_ref, w)
    for rows in chunks():
        put_weighed(stack, rows, grad[rows], depth_ref, 0, True)
    grads[0:16] = grads_ref[...]
    grads[16:32] = jnp.zeros((16, HALF), F32)
    where = [11 + t if t < 5 else 23 + t for t in range(9)]
    moved[...] = dot(near_long_ref[...], slots_ref[:, :HALF])
    depth_rows(grad, moved, grads, where)
    tail, last = grads[16:32], grads[0:16].astype(BF)
    for g in range(PLANE):
        out_ref[g, 0:16] = (point0[16 * g : 16 * g + 16] + tail).astype(BF)
        out_ref[g, 48:64] = last
    grad[...] = dot(near_ref[...], stack[...])
    for rows in chunks():
        tile_grad = jnp.where(live_at(side_ref, rows), masked_ref[rows] + grad[rows], 0.0)
        stack[rows] = tile_grad.astype(BF)
    proj = dot_tn(slots_ref[:, HALF:], stack[0:ALL]).astype(BF)
    for g in range(PLANE):
        out_ref[g, 32:48] = proj[16 * g : 16 * g + 16]


def finish(in_ref, proj_ref, point_ref, depth_ref, bias_ref):
    sums = []
    for r in range(0, 64, 16):
        total = in_ref[0, r : r + 16].astype(F32)
        for g in range(1, PLANE):
            total = total + in_ref[g, r : r + 16].astype(F32)
        sums.append(total)
    proj_ref[...] = sums[2]
    for layer in range(2):
        for i in range(COLS):
            point_ref[i, layer : layer + 1] = sums[layer][i : i + 1]
    for t in range(9):
        depth_ref[t, 0:1] = sums[3][11 + t : 12 + t] if t < 5 else sums[0][7 + t : 8 + t]
        depth_ref[t, 1:2] = sums[3][t : t + 1]
    bias_ref[1:2] = sums[3][9:10]
    bias_ref[0:1] = sums[3][10:11]


def call(body, outs, specs, *args, scratch=(), out_specs=None, mib=20):
    return pl.pallas_call(
        body, out_shape=[jax.ShapeDtypeStruct(s, d) for s, d in outs], in_specs=specs,
        out_specs=out_specs or [VM] * len(outs), scratch_shapes=list(scratch),
        compiler_params=pltpu.CompilerParams(vmem_limit_bytes=mib * 1024 * 1024),
        name=body.__name__)(*args)


def swap(value):
    return lax.ppermute(value, "pipe", [(0, 1), (1, 0)])


def shards(tiles, counts, cells, block_in, block_out, proj, depth, point, bias, cotangent):
    depth = depth.transpose(1, 0, 2)
    x = tiles.reshape(ROWS * POS, CH)
    x, own_side, code = call(
        first_section, [(x.shape, BF), ((NZ, ROWS, SIDE), BF), ((ROWS, 128), BF)],
        [SM, SM] + [HB] * 4, cells, counts.T, cotangent, x, block_in, block_out, mib=60,
        out_specs=[VM, HB, VM],
        scratch=[pltpu.VMEM(cotangent.shape, BF), pltpu.VMEM((NZ, ROWS, SIDE), BF),
                 pltpu.VMEM(x.shape, BF), pltpu.VMEM((CH, 512), BF), pltpu.VMEM((512, CH), BF),
                 pltpu.SemaphoreType.DMA((4, 4))])
    x = lax.ppermute(x, "pipe", [(0, 1)])
    side = lax.all_to_all(own_side, "z", 0, 0, tiled=True).reshape(ALL, SIDE)
    (mine,) = call(second_section, [((ROWS, CH), BF)], [VM, HB, HB], x, block_in, block_out,
                   scratch=[pltpu.VMEM((CH, 512), BF), pltpu.VMEM((512, CH), BF),
                            pltpu.SemaphoreType.DMA((2, 2))], mib=52)
    got = lax.ppermute(mine, "pipe", [(1, 0)])
    (slots,) = call(
        project, [((NZ, ROWS, WIDTH), BF)], [VM] * 4, code, mine, got, proj, out_specs=[HB],
        scratch=[pltpu.VMEM((NZ, ROWS, WIDTH), BF), pltpu.SemaphoreType.DMA((2,))])
    slots = lax.all_to_all(slots, "z", 0, 0, tiled=True).reshape(ALL, WIDTH)
    half_b, half_f = ((ALL, HALF), BF), ((ALL, HALF), F32)
    hits, long_hits = ((ALL, 9 * ALL), BF), ((9 * ALL, ALL), BF)
    near, near_long, far, far_long = call(
        taps, [hits, long_hits, hits, long_hits], [VM], side)
    stack = pltpu.VMEM((9 * ALL, HALF), BF)
    moved, grad = pltpu.VMEM((9 * ALL, HALF), F32), pltpu.VMEM((ALL, HALF), F32)
    sem = pltpu.SemaphoreType.DMA
    spread0, part, send, point1 = call(
        layer0, [half_b, half_f, half_b, ((HALF, FEAT), BF)], [VM] * 3 + [HB], slots, depth, near,
        point, scratch=[stack, pltpu.VMEM((HALF, FEAT), BF), pltpu.SemaphoreType.DMA((2,))],
        mib=48)
    pre0, grid1, spread1, part, send = call(
        layer1, [half_f, half_b, half_b, half_f, half_b], [VM] * 8,
        slots, side, part, swap(send), depth, bias, far, point1, scratch=[stack])
    mixed, slope1, sum1 = call(
        head, [((MB, 1, CELLS, HALF), BF), half_b, ((1, HALF), F32)], [VM] * 5,
        side, part, swap(send), grid1, bias, out_specs=[HB, VM, VM],
        scratch=[pltpu.VMEM((MB, 1, CELLS, HALF), BF), sem])
    got1 = swap(slope1)
    masked, slope0, grads = call(
        back1, [half_f, half_b, ((16, HALF), F32)], [VM] * 10,
        side, slope1, got1, grid1, pre0, sum1, depth, far, far_long, point1,
        scratch=[stack, moved, grad])
    (sums,) = call(
        back0, [((PLANE, 64, HALF), BF)], [VM] * 13 + [HB],
        slots, side, slope0, swap(slope0), slope1, got1, spread0, spread1, masked, grads, depth,
        near, near_long, point,
        scratch=[stack, moved, grad, pltpu.VMEM((32, HALF), F32), pltpu.VMEM((HALF, FEAT), BF), sem],
        mib=40)
    sums = lax.all_to_all(sums, ("y", "x"), 0, 0, tiled=True)
    grad_proj, grad_point, grad_depth, grad_bias = call(
        finish, [((16, HALF), F32), ((COLS, 2, HALF), F32), ((9, 2, HALF), F32), ((2, HALF), F32)],
        [VM], sums)
    return (mixed, grad_proj, grad_point.transpose(1, 2, 0), grad_depth.transpose(1, 0, 2), grad_bias)


def solution(mesh):
    grid = Mesh(mesh.devices.reshape(2, NZ, NY, NX), ("pipe", "z", "y", "x"))
    dp = ("z", "y", "x")
    in_specs = (
        P(None, dp, None, None, None),
        P(None, dp),
        P(None, dp, None),
        P("pipe", None, None),
        P("pipe", None, None),
        P(None, "pipe"),
        P(None, None, "pipe"),
        P(None, "pipe", None),
        P(None, "pipe"),
        P(None, dp, None, "pipe"),
    )
    out_specs = (
        P(None, dp, None, "pipe"),
        P(dp, "pipe"),
        P(None, "pipe", dp),
        P(None, None, "pipe"),
        P(None, "pipe"),
    )
    return jax.shard_map(shards, mesh=grid, in_specs=in_specs, out_specs=out_specs, check_vma=False)
```
